32 devices in a mesh: groups: 2 (over x), ctx: 16 (over z, y, core).
Axes of the slice: x: 2, y: 2, z: 4, core: 2. Of those that a mesh axis runs over, the one named last changes fastest.
Arguments:
- queries: bfloat16 [8192, 2048], P(('groups', 'ctx')), parts along dimension 0, may hold values from -6 to 6
- keys: bfloat16 [8192, 2048], P(('groups', 'ctx')), parts along dimension 0, may hold values from -5 to 5
- values: bfloat16 [8192, 2048], P(('groups', 'ctx')), parts along dimension 0, may hold values from -6 to 6
- bar_lengths: int32 [32], P('groups'), parts along dimension 0, may hold values from 32 to 256, as said below
Outputs:
- attended: bfloat16 [8192, 2048], P(('groups', 'ctx')), parts along dimension 0
The draws below stay inside these ranges and needn't reach their ends.
There are 2 independent parts, one for each index of `groups`. The reference program is written for one: setup_inputs(seed, part) draws one part's arguments, and reference() takes and returns one part's arrays. A program takes and returns all parts, laid end to end along the dimension named above; each array names one. Nothing has to cross between parts.
Inputs may be any that keep to these rules, and one draw needn't show every extreme that they name: `bar_lengths`: used tokens of each bar; the rest of its 256 slots are padding.
All inputs are finite; a program needn't handle non-finite values.
Results may differ from the reference program's by a relative error of at most 0.0038.
Values may be sent and summed in bfloat16 or wider, within the bound.
A program may use at most 128 MiB of HBM per device.

```python
import math
import jax
import jax.numpy as jnp
from jax import lax

H = 16
HD = 128
BAR = 256
NBARS = 16
SEQ = 4096


def draw_queries(key, part):
    key = jax.random.fold_in(key, 1)
    base = 1.5 * jnp.clip(jax.random.normal(key, (NBARS, BAR, H * HD), jnp.float32), -4.0, 4.0)
    return base.reshape(NBARS * BAR, H * HD).astype(jnp.bfloat16)


def draw_keys(key, part):
    key = jax.random.fold_in(key, 2)
    base = jnp.clip(jax.random.normal(key, (NBARS, BAR, H * HD), jnp.float32), -5.0, 5.0)
    return base.reshape(NBARS * BAR, H * HD).astype(jnp.bfloat16)


def draw_bar_lengths(key, part):
    key = jax.random.fold_in(key, 11)
    first, second = jax.random.split(key)
    lengths = jax.random.randint(first, (NBARS,), BAR // 8, BAR + 1)
    longest = jax.random.randint(second, (), 0, NBARS)
    return jnp.where(jnp.arange(NBARS) == longest, BAR, lengths).astype(jnp.int32)


def shard_levels(stream_key, dims, cuts, least, top_value):
    def one(dim, shards_of):
        heights = jax.random.uniform(jax.random.fold_in(jax.random.fold_in(stream_key, 6), dim), (shards_of,), jnp.float32, least / len(cuts), top_value / len(cuts))
        return jnp.repeat(jnp.exp(heights), dims[dim] // shards_of).reshape((-1,) + (1,) * (len(dims) - dim - 1))

    factor_of = one(*cuts[0])
    for cut in cuts[1:]:
        factor_of = factor_of * one(*cut)
    return factor_of


def gaussian(stream_key, dims, spread, limit, shards=(), kind=jnp.bfloat16):
    factor_of = shard_levels(stream_key, dims, shards, -0.22, 0.18) if shards else 1.0
    array = jax.random.normal(stream_key, dims, jnp.float32) * spread * factor_of
    return jnp.minimum(jnp.maximum(array, -limit), limit).astype(kind)


def setup_inputs(seed: int = 0, part: int = 0) -> dict:
    seeds = jax.random.split(jax.random.key(seed), 5)
    part_keys = jax.random.split(jax.random.fold_in(seeds[4], part), 5)
    queries = draw_queries(jax.random.fold_in(jax.random.fold_in(seeds[4], part), 71), part)
    keys = draw_keys(jax.random.fold_in(jax.random.fold_in(seeds[4], part), 71), part)
    values = gaussian(part_keys[2], (SEQ, H * HD), 1.0, 6.0, ((0, 16),))
    bar_lengths = draw_bar_lengths(jax.random.fold_in(jax.random.fold_in(seeds[4], part), 71), part)
    return dict(queries=queries, keys=keys, values=values, bar_lengths=bar_lengths)


BAR_OFFSETS = (1, 2, 4, 8, 12, 16, 24, 32)
NEG_FILL = -1e+30

def reference(queries, keys, values, bar_lengths):
    features = H * HD
    key_bars = keys.reshape(NBARS, BAR, features)
    value_bars = values.reshape(NBARS, BAR, features)
    positions = jnp.arange(BAR, dtype=jnp.int32)
    live_rows = (positions[None, :] < bar_lengths[:, None]).astype(jnp.float32)
    factor = lax.rsqrt(bar_lengths.astype(jnp.float32))[:, None]
    summary_keys = (jnp.einsum('bt,btw->bw', live_rows, key_bars.astype(jnp.float32)) * factor).astype(jnp.bfloat16)
    summary_values = (jnp.einsum('bt,btw->bw', live_rows, value_bars.astype(jnp.float32)) * factor).astype(jnp.bfloat16)
    all_bars = jnp.arange(NBARS, dtype=jnp.int32)

    def one_bar(bar_index):
        query_rows = lax.dynamic_slice_in_dim(queries, (bar_index * BAR).astype(jnp.int32), BAR, 0)
        own_len = bar_lengths[bar_index]
        key_parts = [key_bars[bar_index]]
        value_parts = [value_bars[bar_index]]
        mask_parts = [(positions[None, :] <= positions[:, None]) & (positions[None, :] < own_len)]
        coarse = all_bars < bar_index
        for offset in BAR_OFFSETS:
            source_bar = bar_index - offset
            clamped = jnp.maximum(source_bar, 0).astype(jnp.int32)
            near_len = jnp.where(source_bar >= 0, bar_lengths[clamped], 0)
            key_parts.append(key_bars[clamped])
            value_parts.append(value_bars[clamped])
            mask_parts.append(jnp.broadcast_to((positions < near_len)[None, :], (BAR, BAR)))
            coarse = coarse & (all_bars != source_bar)
        key_parts.append(summary_keys)
        value_parts.append(summary_values)
        mask_parts.append(jnp.broadcast_to(coarse[None, :], (BAR, NBARS)))
        key_rows = jnp.concatenate(key_parts, 0).astype(jnp.float32).reshape(-1, H, HD)
        value_rows = jnp.concatenate(value_parts, 0).astype(jnp.float32).reshape(-1, H, HD)
        key_mask = jnp.concatenate(mask_parts, 1)
        query_heads = query_rows.astype(jnp.float32).reshape(BAR, H, HD)
        scores = jnp.einsum('qhd,khd->hqk', query_heads, key_rows) * (1.0 / math.sqrt(HD))
        scores = jnp.where(key_mask[None], scores, NEG_FILL)
        row_max = lax.optimization_barrier(jnp.max(scores, axis=2, keepdims=True))
        weights = jnp.where(key_mask[None], jnp.exp(scores - row_max), 0.0)
        row_total = lax.optimization_barrier(jnp.sum(weights, axis=2))
        rounded = lax.optimization_barrier(weights.astype(jnp.bfloat16)).astype(jnp.float32)
        mixed = jnp.einsum('hqk,khd->qhd', rounded, value_rows) / jnp.transpose(row_total)[:, :, None]
        mixed = mixed * (positions < own_len).astype(jnp.float32)[:, None, None]
        return mixed.reshape(BAR, features).astype(jnp.bfloat16)
    return lax.map(one_bar, all_bars).reshape(NBARS * BAR, features)
```

```python
import functools
import math

import jax
import jax.numpy as jnp
from jax import lax
from jax.experimental import pallas as pl
from jax.experimental.pallas import tpu as pltpu
from jax.sharding import PartitionSpec as P

HD = 128
BAR_OFFSETS = (1, 2, 4, 8, 12, 16, 24, 32)
NEG_FILL = -1e30
LOG2E = math.log2(math.e)
SCALE = LOG2E / math.sqrt(HD)
CHUNKS = 4
AHEAD = 1
STRIDE = 4


def kernel(
    nb, hops, chunks, len_ref, q_ref, k_ref, v_ref, o_ref,
    qin, oin, osend, lin, lsend, acc, mst, lst, sum_f32, sum_send, sum_in, sum_wide, sum_rows,
    q_send, q_recv, o_send, o_recv, l_send, l_recv, s_send, s_recv,
):
    rows, features = q_ref.shape
    heads = features // HD
    width = features // chunks
    per = width // HD
    near2, near1 = hops, hops + 1
    slots = hops + 2
    me = lax.axis_index("ctx")
    low_half = lax.rem(lax.div(me, 2), 2) == 0
    even = lax.rem(me, 2) == 0
    own_len = len_ref[me]

    def columns(c):
        return pl.ds(pl.multiple_of(c * width, width), width)

    def exists(slot):
        far = me + STRIDE * (slot + 1) < nb
        return jnp.where(slot == near2, me + 2 < nb, jnp.where(slot == near1, me + 1 < nb, far))

    def parent(slot):
        two = jnp.where(low_half, me + 2, me - 2)
        one = jnp.where(even, me + 1, me - 1)
        return jnp.where(slot == near2, two, jnp.where(slot == near1, one, me + STRIDE))

    def q_copy(src, slot, c, target):
        return pltpu.make_async_remote_copy(
            src_ref=src, dst_ref=qin.at[slot, c], send_sem=q_send.at[slot, c],
            recv_sem=q_recv.at[slot, c], device_id={"ctx": target},
            device_id_type=pl.DeviceIdType.MESH,
        )

    def o_copies(slot, c, target):
        return (
            pltpu.make_async_remote_copy(
                src_ref=osend.at[slot, c], dst_ref=oin.at[slot, c], send_sem=o_send.at[slot, c],
                recv_sem=o_recv.at[slot, c], device_id={"ctx": target},
                device_id_type=pl.DeviceIdType.MESH,
            ),
            pltpu.make_async_remote_copy(
                src_ref=lsend.at[slot, c], dst_ref=lin.at[slot, c], send_sem=l_send.at[slot, c],
                recv_sem=l_recv.at[slot, c], device_id={"ctx": target},
                device_id_type=pl.DeviceIdType.MESH,
            ),
        )

    def s_copy(target):
        return pltpu.make_async_remote_copy(
            src_ref=sum_send, dst_ref=sum_in.at[me], send_sem=s_send.at[target],
            recv_sem=s_recv.at[me], device_id={"ctx": target},
            device_id_type=pl.DeviceIdType.MESH,
        )

    sum_in[...] = jnp.zeros_like(sum_in)
    barrier = pltpu.get_barrier_semaphore()

    @pl.loop(0, nb)
    def _(j):
        @pl.when(j != me)
        def _():
            pl.semaphore_signal(
                barrier, inc=1, device_id={"ctx": j}, device_id_type=pl.DeviceIdType.MESH
            )

    live = (lax.broadcasted_iota(jnp.int32, (16, rows), 1) < own_len).astype(jnp.bfloat16)
    factor = lax.rsqrt(jnp.full((1, HD), own_len, jnp.int32).astype(jnp.float32))
    for part, ref in enumerate((k_ref, v_ref)):
        for h in range(heads):
            pooled = jnp.dot(
                live, ref[:, h * HD : (h + 1) * HD], preferred_element_type=jnp.float32
            )
            sum_f32[part * heads + h : part * heads + h + 1, :] = pooled[0:1, :] * factor
    sum_send[...] = sum_f32[...].astype(jnp.bfloat16)

    pl.semaphore_wait(barrier, nb - 1)

    for c in range(chunks):
        source = q_ref.at[:, c * width : (c + 1) * width]

        @pl.when(me >= STRIDE)
        def _():
            q_copy(source, 0, c, me - STRIDE).start()

        @pl.when(jnp.logical_not(low_half))
        def _():
            q_copy(source, near2, c, me - 2).start()

        @pl.when(jnp.logical_not(even))
        def _():
            q_copy(source, near1, c, me - 1).start()

        if c == 0:
            @pl.loop(0, nb)
            def _(j):
                @pl.when(j > me)
                def _():
                    s_copy(j).start()

    def forward(c):
        for slot in range(slots):
            @pl.when(exists(slot))
            def _(slot=slot):
                q_copy(qin.at[slot, c], slot, c, parent(slot)).wait_recv()
                if slot + 1 < hops:
                    @pl.when(me >= STRIDE)
                    def _():
                        q_copy(qin.at[slot, c], slot + 1, c, me - STRIDE).start()
                if slot == 0:
                    @pl.when(low_half)
                    def _():
                        q_copy(qin.at[slot, c], near2, c, me + 2).start()
                if slot == near2:
                    @pl.when(even)
                    def _():
                        q_copy(qin.at[slot, c], near1, c, me + 1).start()

    lane = lax.broadcasted_iota(jnp.int32, (rows, HD), 1)
    key_pos = lax.broadcasted_iota(jnp.int32, (1, rows), 1)
    live_bias = jnp.where(key_pos < own_len, 0.0, NEG_FILL).astype(jnp.float32)

    def scores_of(q, k):
        return lax.dot_general(
            q, k, (((1,), (1,)), ((), ())), preferred_element_type=jnp.float32
        ) * SCALE

    def head_columns(c, h):
        return pl.ds(pl.multiple_of(c * width + h * HD, HD), HD)

    def local_peer(slot, c):
        m_all = jnp.zeros((rows, HD), jnp.float32)
        l_all = jnp.ones((rows, HD), jnp.float32)
        for h in range(per):
            here = slice(h * HD, (h + 1) * HD)
            s = scores_of(qin[slot, c, :, here], k_ref[:, head_columns(c, h)]) + live_bias
            m = jnp.max(s, axis=1, keepdims=True)
            p = jnp.exp2(s - m)
            l = jnp.sum(p, axis=1, keepdims=True)
            acc[:, here] = jnp.dot(
                p.astype(jnp.bfloat16), v_ref[:, head_columns(c, h)],
                preferred_element_type=jnp.float32,
            )
            m_all = jnp.where(lane == h, m, m_all)
            l_all = jnp.where(lane == h, l, l_all)
        mst[...] = m_all
        lst[...] = l_all

    def local_own(c):
        causal = (
            lax.broadcasted_iota(jnp.int32, (rows, rows), 1)
            <= lax.broadcasted_iota(jnp.int32, (rows, rows), 0)
        ) & (key_pos < own_len)
        bars = lax.broadcasted_iota(jnp.int32, (1, nb), 1)
        coarse = bars < me
        for offset in BAR_OFFSETS:
            coarse = coarse & (bars != me - offset)
        coarse_bias = jnp.where(coarse, 0.0, NEG_FILL).astype(jnp.float32)
        m_all = jnp.zeros((rows, HD), jnp.float32)
        l_all = jnp.ones((rows, HD), jnp.float32)
        for h in range(per):
            here = slice(h * HD, (h + 1) * HD)
            q = q_ref[:, head_columns(c, h)]
            s = jnp.where(causal, scores_of(q, k_ref[:, head_columns(c, h)]), NEG_FILL)
            t = scores_of(q, sum_rows[0, :, head_columns(c, h)]) + coarse_bias
            m = jnp.maximum(
                jnp.max(s, axis=1, keepdims=True), jnp.max(t, axis=1, keepdims=True)
            )
            p = jnp.exp2(s - m)
            r = jnp.exp2(t - m)
            l = jnp.sum(p, axis=1, keepdims=True) + jnp.sum(r, axis=1, keepdims=True)
            acc[:, here] = jnp.dot(
                p.astype(jnp.bfloat16), v_ref[:, head_columns(c, h)],
                preferred_element_type=jnp.float32,
            ) + jnp.dot(
                r.astype(jnp.bfloat16), sum_rows[1, :, head_columns(c, h)],
                preferred_element_type=jnp.float32,
            )
            m_all = jnp.where(lane == h, m, m_all)
            l_all = jnp.where(lane == h, l, l_all)
        mst[...] = m_all
        lst[...] = l_all

    def merge(slot, c):
        for copy in o_copies(slot, c, parent(slot)):
            copy.wait_recv()
        padded = jnp.concatenate(
            [lin[slot, c], jnp.zeros((HD - lin.shape[2], rows), jnp.float32)], axis=0
        )
        theirs = jnp.transpose(padded)
        mine = mst[...]
        top = jnp.maximum(mine, theirs)
        keep = jnp.exp2(mine - top)
        add = jnp.exp2(theirs - top)
        mst[...] = top
        lst[...] = lst[...] * keep + add
        for h in range(per):
            here = slice(h * HD, (h + 1) * HD)
            acc[:, here] = (
                acc[:, here] * keep[:, h : h + 1]
                + oin[slot, c, :, here].astype(jnp.float32) * add[:, h : h + 1]
            )

    idle_hops = [s for s in range(hops) if STRIDE * (s + 1) not in BAR_OFFSETS]

    def answer(slot, c):
        if idle_hops:
            idle = functools.reduce(jnp.logical_or, [slot == s for s in idle_hops])

            @pl.when(idle)
            def _():
                acc[...] = jnp.zeros_like(acc)
                mst[...] = jnp.full_like(mst, NEG_FILL)
                lst[...] = jnp.ones_like(lst)

            @pl.when(jnp.logical_not(idle))
            def _():
                local_peer(slot, c)
        else:
            local_peer(slot, c)

        @pl.when((slot + 1 < hops) & (me >= STRIDE))
        def _():
            merge(jnp.minimum(slot + 1, hops - 1), c)

        @pl.when((slot == 0) & low_half)
        def _():
            merge(near2, c)

        @pl.when((slot == near2) & even)
        def _():
            merge(near1, c)

        total = lst[...]
        inverse = 1.0 / total
        for h in range(per):
            here = slice(h * HD, (h + 1) * HD)
            osend[slot, c, :, here] = (acc[:, here] * inverse[:, h : h + 1]).astype(jnp.bfloat16)
        level = mst[...] + jnp.log(total) * LOG2E
        lsend[slot, c] = jnp.transpose(level)[: lsend.shape[2], :]
        for copy in o_copies(slot, c, parent(slot)):
            copy.start()

    def finish(c):
        local_own(c)

        @pl.when(me >= STRIDE)
        def _():
            merge(0, c)

        @pl.when(jnp.logical_not(low_half))
        def _():
            merge(near2, c)

        @pl.when(jnp.logical_not(even))
        def _():
            merge(near1, c)

        used = lax.broadcasted_iota(jnp.int32, (rows, HD), 0) < own_len
        inverse = jnp.where(used, 1.0 / lst[...], 0.0)
        for h in range(per):
            o_ref[:, head_columns(c, h)] = (
                acc[:, h * HD : (h + 1) * HD] * inverse[:, h : h + 1]
            ).astype(o_ref.dtype)

    for c in range(min(AHEAD, chunks)):
        forward(c)

    @pl.loop(0, nb)
    def _(j):
        @pl.when(j < me)
        def _():
            pltpu.make_async_remote_copy(
                src_ref=sum_send, dst_ref=sum_in.at[j], send_sem=s_send.at[j],
                recv_sem=s_recv.at[j], device_id={"ctx": j},
                device_id_type=pl.DeviceIdType.MESH,
            ).wait_recv()

    sum_wide[...] = sum_in[...].astype(jnp.float32)
    for part in range(2):
        for h in range(heads):
            sum_rows[part, :, h * HD : (h + 1) * HD] = sum_wide[:, part * heads + h, :].astype(
                jnp.bfloat16
            )

    @pl.loop(0, chunks + 1)
    def _(step):
        @pl.when(step + AHEAD < chunks)
        def _():
            forward(step + AHEAD)

        @pl.when(step < chunks)
        def _():
            @pl.loop(0, slots)
            def _(j):
                slot = slots - 1 - j

                @pl.when(exists(slot))
                def _():
                    answer(slot, step)

        @pl.when(step >= 1)
        def _():
            finish(step - 1)

    @pl.loop(0, nb)
    def _(j):
        @pl.when(j > me)
        def _():
            s_copy(j).wait_send()

    @pl.loop(0, chunks)
    def _(c):
        for slot in range(slots):
            if slot == 0:
                sent = me >= STRIDE
            elif slot < hops:
                sent = (me >= STRIDE) & (me + STRIDE * slot < nb)
            elif slot == near2:
                sent = jnp.logical_not(low_half) | (me + STRIDE < nb)
            else:
                sent = jnp.logical_not(even) | (me + 2 < nb)

            @pl.when(sent)
            def _(slot=slot):
                q_copy(qin.at[slot, c], slot, c, parent(slot)).wait_send()

            @pl.when(exists(slot))
            def _(slot=slot):
                for copy in o_copies(slot, c, parent(slot)):
                    copy.wait_send()


def local(queries, keys, values, bar_lengths):
    nb = lax.axis_size("ctx")
    rows, features = queries.shape
    heads = features // HD
    chunks = CHUNKS
    width = features // chunks
    hops = max(o // STRIDE for o in BAR_OFFSETS if o % STRIDE == 0 and o < nb)
    slots = hops + 2
    stat_rows = 8
    piece = (slots, chunks, rows, width)
    sems = pltpu.SemaphoreType.DMA((slots, chunks))
    whole = pl.BlockSpec(memory_space=pltpu.VMEM)
    return pl.pallas_call(
        functools.partial(kernel, nb, hops, chunks),
        out_shape=jax.ShapeDtypeStruct((rows, features), jnp.bfloat16),
        in_specs=[pl.BlockSpec(memory_space=pltpu.SMEM), whole, whole, whole],
        out_specs=whole,
        scratch_shapes=[
            pltpu.VMEM(piece, jnp.bfloat16),
            pltpu.VMEM(piece, jnp.bfloat16),
            pltpu.VMEM(piece, jnp.bfloat16),
            pltpu.VMEM((slots, chunks, stat_rows, rows), jnp.float32),
            pltpu.VMEM((slots, chunks, stat_rows, rows), jnp.float32),
            pltpu.VMEM((rows, width), jnp.float32),
            pltpu.VMEM((rows, HD), jnp.float32),
            pltpu.VMEM((rows, HD), jnp.float32),
            pltpu.VMEM((2 * heads, HD), jnp.float32),
            pltpu.VMEM((2 * heads, HD), jnp.bfloat16),
            pltpu.VMEM((nb, 2 * heads, HD), jnp.bfloat16),
            pltpu.VMEM((nb, 2 * heads, HD), jnp.float32),
            pltpu.VMEM((2, nb, features), jnp.bfloat16),
            sems, sems, sems, sems, sems, sems,
            pltpu.SemaphoreType.DMA((nb,)),
            pltpu.SemaphoreType.DMA((nb,)),
        ],
        compiler_params=pltpu.CompilerParams(
            collective_id=0, has_side_effects=True, vmem_limit_bytes=56 * 2**20
        ),
        name="bar_attention",
    )(bar_lengths, queries, keys, values)


def solution(mesh):
    placed = (
        P(("groups", "ctx"), None),
        P(("groups", "ctx"), None),
        P(("groups", "ctx"), None),
        P("groups"),
    )
    return jax.shard_map(
        local, mesh=mesh, in_specs=placed, out_specs=P(("groups", "ctx"), None), check_vma=False
    )
```

```python
import functools
import math

import jax
import jax.numpy as jnp
from jax import lax
from jax.experimental import pallas as pl
from jax.experimental.pallas import tpu as pltpu
from jax.sharding import PartitionSpec as P

HD = 128
BAR_OFFSETS = (1, 2, 4, 8, 12, 16, 24, 32)
NEG_FILL = -1e30
LOG2E = math.log2(math.e)
SCALE = LOG2E / math.sqrt(HD)
CHUNKS = 8
EARLY = 1
LAG_NEAR = 1
LAG_EDGE = 2
LAG_FAR = 2
LAG_HOP = 1
STRIDE = 4


def kernel(
    nb, hops, chunks, len_ref, q_ref, k_ref, v_ref, o_ref,
    qin, oin, osend, lin, lloc, held, acc, sum_f32, sum_send, sum_in, sum_wide, sum_rows,
    q_send, q_recv, o_send, o_recv, l_send, l_recv, s_send, s_recv,
):
    rows, features = q_ref.shape
    heads = features // HD
    width = features // chunks
    per = width // HD
    near2, near1 = hops, hops + 1
    slots = hops + 2
    own, own_held = slots, hops - 1
    me = lax.axis_index("ctx")
    low_half = lax.rem(lax.div(me, 2), 2) == 0
    even = lax.rem(me, 2) == 0
    own_len = len_ref[me]

    def columns(c):
        return pl.ds(pl.multiple_of(c * width, width), width)

    def exists(slot):
        far = me + STRIDE * (slot + 1) < nb
        return jnp.where(slot == near2, me + 2 < nb, jnp.where(slot == near1, me + 1 < nb, far))

    def parent(slot):
        two = jnp.where(low_half, me + 2, me - 2)
        one = jnp.where(even, me + 1, me - 1)
        return jnp.where(slot == near2, two, jnp.where(slot == near1, one, me + STRIDE))

    def q_copy(src, slot, c, target):
        return pltpu.make_async_remote_copy(
            src_ref=src, dst_ref=qin.at[slot, c], send_sem=q_send.at[slot, c],
            recv_sem=q_recv.at[slot, c], device_id={"ctx": target},
            device_id_type=pl.DeviceIdType.MESH,
        )

    def o_copies(slot, c, target):
        return (
            pltpu.make_async_remote_copy(
                src_ref=osend.at[slot, c], dst_ref=oin.at[slot, c], send_sem=o_send.at[slot, c],
                recv_sem=o_recv.at[slot, c], device_id={"ctx": target},
                device_id_type=pl.DeviceIdType.MESH,
            ),
            pltpu.make_async_remote_copy(
                src_ref=lloc.at[slot, c], dst_ref=lin.at[slot, c], send_sem=l_send.at[slot, c],
                recv_sem=l_recv.at[slot, c], device_id={"ctx": target},
                device_id_type=pl.DeviceIdType.MESH,
            ),
        )

    def s_copy(target):
        return pltpu.make_async_remote_copy(
            src_ref=sum_send, dst_ref=sum_in.at[me], send_sem=s_send.at[target],
            recv_sem=s_recv.at[me], device_id={"ctx": target},
            device_id_type=pl.DeviceIdType.MESH,
        )

    sum_in[...] = jnp.zeros_like(sum_in)
    barrier = pltpu.get_barrier_semaphore()

    @pl.loop(0, nb)
    def _(j):
        @pl.when(j != me)
        def _():
            pl.semaphore_signal(
                barrier, inc=1, device_id={"ctx": j}, device_id_type=pl.DeviceIdType.MESH
            )

    live = (lax.broadcasted_iota(jnp.int32, (16, rows), 1) < own_len).astype(jnp.bfloat16)
    factor = lax.rsqrt(jnp.full((1, HD), own_len, jnp.int32).astype(jnp.float32))
    for part, ref in enumerate((k_ref, v_ref)):
        for h in range(heads):
            pooled = jnp.dot(
                live, ref[:, h * HD : (h + 1) * HD], preferred_element_type=jnp.float32
            )
            sum_f32[part * heads + h : part * heads + h + 1, :] = pooled[0:1, :] * factor
    sum_send[...] = sum_f32[...].astype(jnp.bfloat16)

    pl.semaphore_wait(barrier, nb - 1)

    def send_own(c):
        source = q_ref.at[:, columns(c)]

        @pl.when(me >= STRIDE)
        def _():
            q_copy(source, 0, c, me - STRIDE).start()

        @pl.when(jnp.logical_not(low_half))
        def _():
            q_copy(source, near2, c, me - 2).start()

        @pl.when(jnp.logical_not(even))
        def _():
            q_copy(source, near1, c, me - 1).start()

    for c in range(min(EARLY, chunks)):
        send_own(c)

    @pl.loop(0, nb)
    def _(j):
        @pl.when(j > me)
        def _():
            s_copy(j).start()

    def forward(c):
        for slot in range(slots):
            @pl.when(exists(slot))
            def _(slot=slot):
                q_copy(qin.at[slot, c], slot, c, parent(slot)).wait_recv()
                if slot + 1 < hops:
                    @pl.when(me >= STRIDE)
                    def _():
                        q_copy(qin.at[slot, c], slot + 1, c, me - STRIDE).start()
                if slot == 0:
                    @pl.when(low_half)
                    def _():
                        q_copy(qin.at[slot, c], near2, c, me + 2).start()
                if slot == near2:
                    @pl.when(even)
                    def _():
                        q_copy(qin.at[slot, c], near1, c, me + 1).start()

            if slot == hops - 1:
                @pl.when(c + EARLY < chunks)
                def _():
                    send_own(c + EARLY)

    lane = lax.broadcasted_iota(jnp.int32, (rows, HD), 1)
    key_pos = lax.broadcasted_iota(jnp.int32, (1, rows), 1)
    live_bias = jnp.where(key_pos < own_len, 0.0, NEG_FILL).astype(jnp.float32)

    def scores_of(q, k):
        return lax.dot_general(
            q, k, (((1,), (1,)), ((), ())), preferred_element_type=jnp.float32
        ) * SCALE

    def head_columns(c, h):
        return pl.ds(pl.multiple_of(c * width + h * HD, HD), HD)

    def keep_state(levels, totals, slot, c):
        inverse = 1.0 / totals
        for h in range(per):
            here = slice(h * HD, (h + 1) * HD)
            acc[:, here] = acc[:, here] * inverse[:, h : h + 1]
        log_sums = levels + jnp.log(totals) * LOG2E
        lloc[slot, c] = jnp.transpose(log_sums)[: lloc.shape[2], :]

    def local_peer(slot, c):
        m_all = jnp.zeros((rows, HD), jnp.float32)
        l_all = jnp.ones((rows, HD), jnp.float32)
        for h in range(per):
            here = slice(h * HD, (h + 1) * HD)
            s = scores_of(qin[slot, c, :, here], k_ref[:, head_columns(c, h)]) + live_bias
            m = jnp.max(s, axis=1, keepdims=True)
            p = jnp.exp2(s - m)
            l = jnp.sum(p, axis=1, keepdims=True)
            acc[:, here] = jnp.dot(
                p.astype(jnp.bfloat16), v_ref[:, head_columns(c, h)],
                preferred_element_type=jnp.float32,
            )
            m_all = jnp.where(lane == h, m, m_all)
            l_all = jnp.where(lane == h, l, l_all)
        keep_state(m_all, l_all, slot, c)

    def local_own(c):
        causal = (
            lax.broadcasted_iota(jnp.int32, (rows, rows), 1)
            <= lax.broadcasted_iota(jnp.int32, (rows, rows), 0)
        ) & (key_pos < own_len)
        bars = lax.broadcasted_iota(jnp.int32, (1, nb), 1)
        coarse = bars < me
        for offset in BAR_OFFSETS:
            coarse = coarse & (bars != me - offset)
        coarse_bias = jnp.where(coarse, 0.0, NEG_FILL).astype(jnp.float32)
        m_all = jnp.zeros((rows, HD), jnp.float32)
        l_all = jnp.ones((rows, HD), jnp.float32)
        for h in range(per):
            here = slice(h * HD, (h + 1) * HD)
            q = q_ref[:, head_columns(c, h)]
            s = jnp.where(causal, scores_of(q, k_ref[:, head_columns(c, h)]), NEG_FILL)
            t = scores_of(q, sum_rows[0, :, head_columns(c, h)]) + coarse_bias
            m = jnp.maximum(
                jnp.max(s, axis=1, keepdims=True), jnp.max(t, axis=1, keepdims=True)
            )
            p = jnp.exp2(s - m)
            r = jnp.exp2(t - m)
            l = jnp.sum(p, axis=1, keepdims=True) + jnp.sum(r, axis=1, keepdims=True)
            acc[:, here] = jnp.dot(
                p.astype(jnp.bfloat16), v_ref[:, head_columns(c, h)],
                preferred_element_type=jnp.float32,
            ) + jnp.dot(
                r.astype(jnp.bfloat16), sum_rows[1, :, head_columns(c, h)],
                preferred_element_type=jnp.float32,
            )
            m_all = jnp.where(lane == h, m, m_all)
            l_all = jnp.where(lane == h, l, l_all)
        keep_state(m_all, l_all, own, c)
        held[own_held, c] = acc[...]

    def merge(child, held_slot, slot, c):
        for copy in o_copies(child, c, parent(child)):
            copy.wait_recv()
        mine, theirs = lloc[slot, c], lin[child, c]
        top = jnp.maximum(mine, theirs)
        both = top + jnp.log(jnp.exp2(mine - top) + jnp.exp2(theirs - top)) * LOG2E
        lloc[slot, c] = both
        shares = jnp.transpose(
            jnp.concatenate(
                [
                    jnp.exp2(mine - both),
                    jnp.exp2(theirs - both),
                    jnp.zeros((HD - 2 * mine.shape[0], rows), jnp.float32),
                ],
                axis=0,
            )
        )
        second = mine.shape[0]
        for h in range(per):
            here = slice(h * HD, (h + 1) * HD)
            held[held_slot, c, :, here] = (
                held[held_slot, c, :, here] * shares[:, h : h + 1]
                + oin[child, c, :, here].astype(jnp.float32) * shares[:, second + h : second + h + 1]
            )

    def send_state(state, slot, c):
        osend[slot, c] = state.astype(jnp.bfloat16)
        for copy in o_copies(slot, c, parent(slot)):
            copy.start()

    idle_hops = [s for s in range(hops) if STRIDE * (s + 1) not in BAR_OFFSETS]
    far_child = me >= STRIDE

    def local_answer(slot, c):
        if idle_hops:
            idle = functools.reduce(jnp.logical_or, [slot == s for s in idle_hops])

            @pl.when(idle)
            def _():
                acc[...] = jnp.zeros_like(acc)
                lloc[slot, c] = jnp.full(lloc.shape[2:], NEG_FILL, jnp.float32)

            @pl.when(jnp.logical_not(idle))
            def _():
                local_peer(slot, c)
        else:
            local_peer(slot, c)

        has_child = (
            ((slot + 1 < hops) & far_child) | ((slot == 0) & low_half) | ((slot == near2) & even)
        )

        @pl.when(jnp.logical_not(has_child))
        def _():
            send_state(acc[...], slot, c)

        @pl.when(has_child)
        def _():
            held[slot, c] = acc[...]

    def finish(c):
        @pl.when(far_child)
        def _():
            merge(0, own_held, own, c)

        @pl.when(jnp.logical_not(low_half))
        def _():
            merge(near2, own_held, own, c)

        @pl.when(jnp.logical_not(even))
        def _():
            merge(near1, own_held, own, c)

        used = lax.broadcasted_iota(jnp.int32, (rows, HD), 0) < own_len
        for h in range(per):
            here = slice(h * HD, (h + 1) * HD)
            o_ref[:, head_columns(c, h)] = jnp.where(
                used, held[own_held, c, :, here], 0.0
            ).astype(o_ref.dtype)

    @pl.loop(0, nb)
    def _(j):
        @pl.when(j < me)
        def _():
            pltpu.make_async_remote_copy(
                src_ref=sum_send, dst_ref=sum_in.at[j], send_sem=s_send.at[j],
                recv_sem=s_recv.at[j], device_id={"ctx": j},
                device_id_type=pl.DeviceIdType.MESH,
            ).wait_recv()

    sum_wide[...] = sum_in[...].astype(jnp.float32)
    for part in range(2):
        for h in range(heads):
            sum_rows[part, :, h * HD : (h + 1) * HD] = sum_wide[:, part * heads + h, :].astype(
                jnp.bfloat16
            )

    far_lags = [LAG_FAR + LAG_HOP * (hops - 2 - s) for s in range(hops - 1)]
    own_lag = (far_lags[0] if far_lags else LAG_FAR) + LAG_HOP

    @pl.loop(0, chunks + 1 + own_lag)
    def _(step):
        def at(lag, also, body):
            c = step - 1 - lag

            @pl.when((c >= 0) & (c < chunks) & also)
            def _():
                body(c)

        @pl.when(step < chunks)
        def _():
            forward(step)

        @pl.when((step >= 1) & (step <= chunks))
        def _():
            @pl.loop(0, slots)
            def _(j):
                slot = slots - 1 - j

                @pl.when(exists(slot))
                def _():
                    local_answer(slot, step - 1)

            local_own(step - 1)

        def near_answer(c):
            merge(near1, near2, near2, c)
            send_state(held[near2, c], near2, c)

        at(LAG_NEAR, exists(near2) & even, near_answer)

        for s in reversed(range(hops)):
            def far_answer(c, s=s):
                merge(s + 1, s, s, c)
                if s == 0:
                    @pl.when(low_half)
                    def _():
                        merge(near2, s, s, c)
                send_state(held[s, c], s, c)

            def edge_answer(c):
                merge(near2, 0, 0, c)
                send_state(held[0, c], 0, c)

            if s < hops - 1:
                at(far_lags[s], exists(s) & far_child, far_answer)
            if s == 0:
                alone = low_half if hops == 1 else low_half & jnp.logical_not(far_child)
                at(LAG_EDGE, exists(0) & alone, edge_answer)

        at(own_lag, me >= 0, finish)

    @pl.loop(0, nb)
    def _(j):
        @pl.when(j > me)
        def _():
            s_copy(j).wait_send()

    @pl.loop(0, chunks)
    def _(c):
        for slot in range(slots):
            if slot == 0:
                sent = me >= STRIDE
            elif slot < hops:
                sent = (me >= STRIDE) & (me + STRIDE * slot < nb)
            elif slot == near2:
                sent = jnp.logical_not(low_half) | (me + STRIDE < nb)
            else:
                sent = jnp.logical_not(even) | (me + 2 < nb)

            @pl.when(sent)
            def _(slot=slot):
                q_copy(qin.at[slot, c], slot, c, parent(slot)).wait_send()

            @pl.when(exists(slot))
            def _(slot=slot):
                for copy in o_copies(slot, c, parent(slot)):
                    copy.wait_send()


def local(queries, keys, values, bar_lengths):
    nb = lax.axis_size("ctx")
    rows, features = queries.shape
    heads = features // HD
    chunks = CHUNKS
    width = features // chunks
    hops = max(o // STRIDE for o in BAR_OFFSETS if o % STRIDE == 0 and o < nb)
    slots = hops + 2
    stat_rows = 8
    piece = (slots, chunks, rows, width)
    sems = pltpu.SemaphoreType.DMA((slots, chunks))
    whole = pl.BlockSpec(memory_space=pltpu.VMEM)
    return pl.pallas_call(
        functools.partial(kernel, nb, hops, chunks),
        out_shape=jax.ShapeDtypeStruct((rows, features), jnp.bfloat16),
        in_specs=[pl.BlockSpec(memory_space=pltpu.SMEM), whole, whole, whole],
        out_specs=whole,
        scratch_shapes=[
            pltpu.VMEM(piece, jnp.bfloat16),
            pltpu.VMEM(piece, jnp.bfloat16),
            pltpu.VMEM(piece, jnp.bfloat16),
            pltpu.VMEM((slots, chunks, stat_rows, rows), jnp.float32),
            pltpu.VMEM((slots + 1, chunks, stat_rows, rows), jnp.float32),
            pltpu.VMEM((hops + 1, chunks, rows, width), jnp.float32),
            pltpu.VMEM((rows, width), jnp.float32),
            pltpu.VMEM((2 * heads, HD), jnp.float32),
            pltpu.VMEM((2 * heads, HD), jnp.bfloat16),
            pltpu.VMEM((nb, 2 * heads, HD), jnp.bfloat16),
            pltpu.VMEM((nb, 2 * heads, HD), jnp.float32),
            pltpu.VMEM((2, nb, features), jnp.bfloat16),
            sems, sems, sems, sems, sems, sems,
            pltpu.SemaphoreType.DMA((nb,)),
            pltpu.SemaphoreType.DMA((nb,)),
        ],
        compiler_params=pltpu.CompilerParams(
            collective_id=0, has_side_effects=True, vmem_limit_bytes=60 * 2**20
        ),
        name="bar_attention",
    )(bar_lengths, queries, keys, values)


def solution(mesh):
    placed = (
        P(("groups", "ctx"), None),
        P(("groups", "ctx"), None),
        P(("groups", "ctx"), None),
        P("groups"),
    )
    return jax.shard_map(
        local, mesh=mesh, in_specs=placed, out_specs=P(("groups", "ctx"), None), check_vma=False
    )
```

```python
import functools
import math

import jax
import jax.numpy as jnp
from jax import lax
from jax.experimental import pallas as pl
from jax.experimental.pallas import tpu as pltpu
from jax.sharding import PartitionSpec as P

HD = 128
BAR_OFFSETS = (1, 2, 4, 8, 12, 16, 24, 32)
NEG_FILL = -1e30
LOG2E = math.log2(math.e)
SCALE = LOG2E / math.sqrt(HD)
CHUNKS = 8
EARLY = 1
LAG_NEAR = 1
LAG_EDGE = 2
LAG_FAR = 2
LAG_HOP = 1
STRIDE = 4


def kernel(
    nb, hops, chunks, len_ref, q_ref, k_ref, v_ref, o_ref,
    qin, oin, osend, lin, lloc, held, acc, low_kv, sum_f32, sum_send, sum_in, sum_wide, sum_rows,
    q_send, q_recv, o_send, o_recv, l_send, l_recv, s_send, s_recv, kv_send, kv_recv,
):
    rows, features = q_ref.shape
    heads = features // HD
    width = features // chunks
    per = width // HD
    near2, near1 = hops, hops + 1
    slots = hops + 2
    own, own_held, extra = slots, hops - 1, slots
    me = lax.axis_index("ctx")
    low_half = lax.rem(lax.div(me, 2), 2) == 0
    even = lax.rem(me, 2) == 0
    own_len = len_ref[me]
    lender = me < STRIDE
    borrower = (me >= STRIDE) & (me < 2 * STRIDE)
    inner = me >= 2 * STRIDE
    direct = lender & jnp.logical_not(low_half)

    def columns(c):
        return pl.ds(pl.multiple_of(c * width, width), width)

    def exists(slot):
        far = (me + STRIDE * (slot + 1) < nb) & jnp.logical_not(lender)
        return jnp.where(slot == near2, me + 2 < nb, jnp.where(slot == near1, me + 1 < nb, far))

    def parent(slot):
        two = jnp.where(low_half | direct, me + 2, me - 2)
        one = jnp.where(even, me + 1, me - 1)
        return jnp.where(slot == near2, two, jnp.where(slot == near1, one, me + STRIDE))

    def q_copy(src, slot, c, target, lane=None):
        return pltpu.make_async_remote_copy(
            src_ref=src, dst_ref=qin.at[slot, c], send_sem=q_send.at[slot if lane is None else lane, c],
            recv_sem=q_recv.at[slot, c], device_id={"ctx": target},
            device_id_type=pl.DeviceIdType.MESH,
        )

    def o_copies(slot, c, target, into=None):
        if into is None:
            into = jnp.where((slot == near2) & direct, extra, slot)
        return (
            pltpu.make_async_remote_copy(
                src_ref=osend.at[slot, c], dst_ref=oin.at[into, c], send_sem=o_send.at[slot, c],
                recv_sem=o_recv.at[into, c], device_id={"ctx": target},
                device_id_type=pl.DeviceIdType.MESH,
            ),
            pltpu.make_async_remote_copy(
                src_ref=lloc.at[slot, c], dst_ref=lin.at[into, c], send_sem=l_send.at[slot, c],
                recv_sem=l_recv.at[into, c], device_id={"ctx": target},
                device_id_type=pl.DeviceIdType.MESH,
            ),
        )

    def s_copy(target):
        return pltpu.make_async_remote_copy(
            src_ref=sum_send, dst_ref=sum_in.at[me], send_sem=s_send.at[target],
            recv_sem=s_recv.at[me], device_id={"ctx": target},
            device_id_type=pl.DeviceIdType.MESH,
        )

    sum_in[...] = jnp.zeros_like(sum_in)
    barrier = pltpu.get_barrier_semaphore()

    @pl.loop(0, nb)
    def _(j):
        @pl.when(j != me)
        def _():
            pl.semaphore_signal(
                barrier, inc=1, device_id={"ctx": j}, device_id_type=pl.DeviceIdType.MESH
            )

    live = (lax.broadcasted_iota(jnp.int32, (16, rows), 1) < own_len).astype(jnp.bfloat16)
    factor = lax.rsqrt(jnp.full((1, HD), own_len, jnp.int32).astype(jnp.float32))
    for part, ref in enumerate((k_ref, v_ref)):
        for h in range(heads):
            pooled = jnp.dot(
                live, ref[:, h * HD : (h + 1) * HD], preferred_element_type=jnp.float32
            )
            sum_f32[part * heads + h : part * heads + h + 1, :] = pooled[0:1, :] * factor
    sum_send[...] = sum_f32[...].astype(jnp.bfloat16)

    pl.semaphore_wait(barrier, nb - 1)

    def kv_copies(c):
        return [
            pltpu.make_async_remote_copy(
                src_ref=ref.at[:, columns(c)], dst_ref=low_kv.at[part, c],
                send_sem=kv_send.at[part, c], recv_sem=kv_recv.at[part, c],
                device_id={"ctx": me + STRIDE}, device_id_type=pl.DeviceIdType.MESH,
            )
            for part, ref in enumerate((k_ref, v_ref))
        ]

    def send_own(c):
        source = q_ref.at[:, columns(c)]

        @pl.when(inner)
        def _():
            q_copy(source, 0, c, me - STRIDE).start()

        @pl.when(borrower & low_half)
        def _():
            q_copy(source, near2, c, me - 2, extra).start()

        @pl.when(lender)
        def _():
            for copy in kv_copies(c):
                copy.start()

        @pl.when(jnp.logical_not(low_half))
        def _():
            q_copy(source, near2, c, me - 2).start()

        @pl.when(jnp.logical_not(even))
        def _():
            q_copy(source, near1, c, me - 1).start()

    for c in range(min(EARLY, chunks)):
        send_own(c)

    @pl.loop(0, nb)
    def _(j):
        @pl.when(j > me)
        def _():
            s_copy(j).start()

    def forward(c):
        for slot in range(slots):
            @pl.when(exists(slot))
            def _(slot=slot):
                q_copy(qin.at[slot, c], slot, c, parent(slot)).wait_recv()
                if slot + 1 < hops:
                    @pl.when(inner)
                    def _():
                        q_copy(qin.at[slot, c], slot + 1, c, me - STRIDE).start()
                if slot == 0:
                    @pl.when(low_half)
                    def _():
                        q_copy(qin.at[slot, c], near2, c, me + 2).start()
                if slot == near2:
                    @pl.when(even)
                    def _():
                        q_copy(qin.at[slot, c], near1, c, me + 1).start()

            if slot == hops - 1:
                @pl.when(c + EARLY < chunks)
                def _():
                    send_own(c + EARLY)

    lane = lax.broadcasted_iota(jnp.int32, (rows, HD), 1)
    key_pos = lax.broadcasted_iota(jnp.int32, (1, rows), 1)
    live_bias = jnp.where(key_pos < own_len, 0.0, NEG_FILL).astype(jnp.float32)

    low_len = len_ref[jnp.maximum(me - STRIDE, 0)]
    low_bias = jnp.where(key_pos < low_len, 0.0, NEG_FILL).astype(jnp.float32)

    def listed(distance):
        return functools.reduce(jnp.logical_or, [distance == o for o in BAR_OFFSETS])

    def scores_of(q, k):
        return lax.dot_general(
            q, k, (((1,), (1,)), ((), ())), preferred_element_type=jnp.float32
        ) * SCALE

    def head_columns(c, h):
        return pl.ds(pl.multiple_of(c * width + h * HD, HD), HD)

    def keep_state(levels, totals, slot, c):
        inverse = 1.0 / totals
        for h in range(per):
            here = slice(h * HD, (h + 1) * HD)
            acc[:, here] = acc[:, here] * inverse[:, h : h + 1]
        log_sums = levels + jnp.log(totals) * LOG2E
        lloc[slot, c] = jnp.transpose(log_sums)[: lloc.shape[2], :]

    def local_peer(slot, c):
        m_all = jnp.zeros((rows, HD), jnp.float32)
        l_all = jnp.ones((rows, HD), jnp.float32)
        for h in range(per):
            here = slice(h * HD, (h + 1) * HD)
            s = scores_of(qin[slot, c, :, here], k_ref[:, head_columns(c, h)]) + live_bias
            m = jnp.max(s, axis=1, keepdims=True)
            p = jnp.exp2(s - m)
            l = jnp.sum(p, axis=1, keepdims=True)
            acc[:, here] = jnp.dot(
                p.astype(jnp.bfloat16), v_ref[:, head_columns(c, h)],
                preferred_element_type=jnp.float32,
            )
            m_all = jnp.where(lane == h, m, m_all)
            l_all = jnp.where(lane == h, l, l_all)
        keep_state(m_all, l_all, slot, c)

    def local_two(slot, c):
        near_bias = live_bias + jnp.where(listed(STRIDE * (slot + 1)), 0.0, NEG_FILL)
        far_bias = low_bias + jnp.where(listed(STRIDE * (slot + 2)), 0.0, NEG_FILL)
        m_all = jnp.zeros((rows, HD), jnp.float32)
        l_all = jnp.ones((rows, HD), jnp.float32)
        for h in range(per):
            here = slice(h * HD, (h + 1) * HD)
            q = qin[slot, c, :, here]
            s = scores_of(q, k_ref[:, head_columns(c, h)]) + near_bias
            t = scores_of(q, low_kv[0, c, :, here]) + far_bias
            m = jnp.max(jnp.maximum(s, t), axis=1, keepdims=True)
            p = jnp.exp2(s - m)
            r = jnp.exp2(t - m)
            l = jnp.sum(p + r, axis=1, keepdims=True)
            acc[:, here] = jnp.dot(
                p.astype(jnp.bfloat16), v_ref[:, head_columns(c, h)],
                preferred_element_type=jnp.float32,
            ) + jnp.dot(
                r.astype(jnp.bfloat16), low_kv[1, c, :, here],
                preferred_element_type=jnp.float32,
            )
            m_all = jnp.where(lane == h, m, m_all)
            l_all = jnp.where(lane == h, l, l_all)
        keep_state(m_all, l_all, slot, c)

    def local_own(c, two):
        causal = (
            lax.broadcasted_iota(jnp.int32, (rows, rows), 1)
            <= lax.broadcasted_iota(jnp.int32, (rows, rows), 0)
        ) & (key_pos < own_len)
        bars = lax.broadcasted_iota(jnp.int32, (1, nb), 1)
        coarse = bars < me
        for offset in BAR_OFFSETS:
            coarse = coarse & (bars != me - offset)
        coarse_bias = jnp.where(coarse, 0.0, NEG_FILL).astype(jnp.float32)
        m_all = jnp.zeros((rows, HD), jnp.float32)
        l_all = jnp.ones((rows, HD), jnp.float32)
        for h in range(per):
            here = slice(h * HD, (h + 1) * HD)
            q = q_ref[:, head_columns(c, h)]
            s = jnp.where(causal, scores_of(q, k_ref[:, head_columns(c, h)]), NEG_FILL)
            t = scores_of(q, sum_rows[0, :, head_columns(c, h)]) + coarse_bias
            m = jnp.maximum(
                jnp.max(s, axis=1, keepdims=True), jnp.max(t, axis=1, keepdims=True)
            )
            if two:
                u = scores_of(q, low_kv[0, c, :, here]) + low_bias
                m = jnp.maximum(m, jnp.max(u, axis=1, keepdims=True))
            p = jnp.exp2(s - m)
            r = jnp.exp2(t - m)
            l = jnp.sum(p, axis=1, keepdims=True) + jnp.sum(r, axis=1, keepdims=True)
            mixed = jnp.dot(
                p.astype(jnp.bfloat16), v_ref[:, head_columns(c, h)],
                preferred_element_type=jnp.float32,
            ) + jnp.dot(
                r.astype(jnp.bfloat16), sum_rows[1, :, head_columns(c, h)],
                preferred_element_type=jnp.float32,
            )
            if two:
                w = jnp.exp2(u - m)
                l = l + jnp.sum(w, axis=1, keepdims=True)
                mixed = mixed + jnp.dot(
                    w.astype(jnp.bfloat16), low_kv[1, c, :, here],
                    preferred_element_type=jnp.float32,
                )
            acc[:, here] = mixed
            m_all = jnp.where(lane == h, m, m_all)
            l_all = jnp.where(lane == h, l, l_all)
        keep_state(m_all, l_all, own, c)
        held[own_held, c] = acc[...]

    def merge(child, held_slot, slot, c):
        for copy in o_copies(min(child, near1), c, parent(min(child, near1)), child):
            copy.wait_recv()
        mine, theirs = lloc[slot, c], lin[child, c]
        top = jnp.maximum(mine, theirs)
        both = top + jnp.log(jnp.exp2(mine - top) + jnp.exp2(theirs - top)) * LOG2E
        lloc[slot, c] = both
        shares = jnp.transpose(
            jnp.concatenate(
                [
                    jnp.exp2(mine - both),
                    jnp.exp2(theirs - both),
                    jnp.zeros((HD - 2 * mine.shape[0], rows), jnp.float32),
                ],
                axis=0,
            )
        )
        second = mine.shape[0]
        for h in range(per):
            here = slice(h * HD, (h + 1) * HD)
            held[held_slot, c, :, here] = (
                held[held_slot, c, :, here] * shares[:, h : h + 1]
                + oin[child, c, :, here].astype(jnp.float32) * shares[:, second + h : second + h + 1]
            )

    def send_state(state, slot, c):
        osend[slot, c] = state.astype(jnp.bfloat16)
        for copy in o_copies(slot, c, parent(slot)):
            copy.start()

    idle_hops = [s for s in range(hops) if STRIDE * (s + 1) not in BAR_OFFSETS]
    far_child = inner

    def local_answer(slot, c):
        double = borrower & (slot < hops)

        @pl.when(double)
        def _():
            local_two(slot, c)

        if idle_hops:
            idle = functools.reduce(jnp.logical_or, [slot == s for s in idle_hops])
            idle = idle & jnp.logical_not(double)

            @pl.when(idle)
            def _():
                acc[...] = jnp.zeros_like(acc)
                lloc[slot, c] = jnp.full(lloc.shape[2:], NEG_FILL, jnp.float32)

            @pl.when(jnp.logical_not(idle | double))
            def _():
                local_peer(slot, c)
        else:
            @pl.when(jnp.logical_not(double))
            def _():
                local_peer(slot, c)

        has_child = (
            ((slot + 1 < hops) & far_child) | ((slot == 0) & low_half) | ((slot == near2) & even)
        )

        @pl.when(jnp.logical_not(has_child))
        def _():
            send_state(acc[...], slot, c)

        @pl.when(has_child)
        def _():
            held[slot, c] = acc[...]

    def finish(c):
        @pl.when(far_child)
        def _():
            merge(0, own_held, own, c)

        @pl.when(jnp.logical_not(low_half))
        def _():
            merge(near2, own_held, own, c)

        @pl.when(jnp.logical_not(even))
        def _():
            merge(near1, own_held, own, c)

        @pl.when(borrower & low_half)
        def _():
            merge(extra, own_held, own, c)

        used = lax.broadcasted_iota(jnp.int32, (rows, HD), 0) < own_len
        for h in range(per):
            here = slice(h * HD, (h + 1) * HD)
            o_ref[:, head_columns(c, h)] = jnp.where(
                used, held[own_held, c, :, here], 0.0
            ).astype(o_ref.dtype)

    @pl.loop(0, nb)
    def _(j):
        @pl.when(j < me)
        def _():
            pltpu.make_async_remote_copy(
                src_ref=sum_send, dst_ref=sum_in.at[j], send_sem=s_send.at[j],
                recv_sem=s_recv.at[j], device_id={"ctx": j},
                device_id_type=pl.DeviceIdType.MESH,
            ).wait_recv()

    sum_wide[...] = sum_in[...].astype(jnp.float32)
    for part in range(2):
        for h in range(heads):
            sum_rows[part, :, h * HD : (h + 1) * HD] = sum_wide[:, part * heads + h, :].astype(
                jnp.bfloat16
            )

    far_lags = [LAG_FAR + LAG_HOP * (hops - 2 - s) for s in range(hops - 1)]
    own_lag = (far_lags[0] if far_lags else LAG_FAR) + LAG_HOP

    @pl.loop(0, chunks + 1 + own_lag)
    def _(step):
        def at(lag, also, body):
            c = step - 1 - lag

            @pl.when((c >= 0) & (c < chunks) & also)
            def _():
                body(c)

        @pl.when(step < chunks)
        def _():
            forward(step)

        @pl.when((step >= 1) & (step <= chunks))
        def _():
            @pl.when(borrower)
            def _():
                for copy in kv_copies(step - 1):
                    copy.wait_recv()

            @pl.loop(0, slots)
            def _(j):
                slot = slots - 1 - j

                @pl.when(exists(slot))
                def _():
                    local_answer(slot, step - 1)

            @pl.when(borrower)
            def _():
                local_own(step - 1, True)

            @pl.when(jnp.logical_not(borrower))
            def _():
                local_own(step - 1, False)

        def near_answer(c):
            merge(near1, near2, near2, c)
            send_state(held[near2, c], near2, c)

        at(LAG_NEAR, exists(near2) & even, near_answer)

        for s in reversed(range(hops)):
            def far_answer(c, s=s):
                merge(s + 1, s, s, c)
                if s == 0:
                    @pl.when(low_half)
                    def _():
                        merge(near2, s, s, c)
                send_state(held[s, c], s, c)

            def edge_answer(c):
                merge(near2, 0, 0, c)
                send_state(held[0, c], 0, c)

            if s < hops - 1:
                at(far_lags[s], exists(s) & far_child, far_answer)
            if s == 0:
                alone = low_half if hops == 1 else low_half & jnp.logical_not(far_child)
                at(LAG_EDGE, exists(0) & alone, edge_answer)

        at(own_lag, me >= 0, finish)

    @pl.loop(0, nb)
    def _(j):
        @pl.when(j > me)
        def _():
            s_copy(j).wait_send()

    @pl.loop(0, chunks)
    def _(c):
        @pl.when(borrower & low_half)
        def _():
            q_copy(qin.at[near2, c], near2, c, me - 2, extra).wait_send()

        @pl.when(lender)
        def _():
            for copy in kv_copies(c):
                copy.wait_send()

        for slot in range(slots):
            if slot == 0:
                sent = inner
            elif slot < hops:
                sent = inner & (me + STRIDE * slot < nb)
            elif slot == near2:
                sent = jnp.logical_not(low_half) | ((me + STRIDE < nb) & jnp.logical_not(lender))
            else:
                sent = jnp.logical_not(even) | (me + 2 < nb)

            @pl.when(sent)
            def _(slot=slot):
                q_copy(qin.at[slot, c], slot, c, parent(slot)).wait_send()

            @pl.when(exists(slot))
            def _(slot=slot):
                for copy in o_copies(slot, c, parent(slot)):
                    copy.wait_send()


def local(queries, keys, values, bar_lengths):
    nb = lax.axis_size("ctx")
    rows, features = queries.shape
    heads = features // HD
    chunks = CHUNKS
    width = features // chunks
    hops = max(o // STRIDE for o in BAR_OFFSETS if o % STRIDE == 0 and o < nb)
    hops = min(hops, nb // STRIDE - 2)
    slots = hops + 2
    stat_rows = 8
    piece = (slots, chunks, rows, width)
    sems = pltpu.SemaphoreType.DMA((slots + 1, chunks))
    whole = pl.BlockSpec(memory_space=pltpu.VMEM)
    return pl.pallas_call(
        functools.partial(kernel, nb, hops, chunks),
        out_shape=jax.ShapeDtypeStruct((rows, features), jnp.bfloat16),
        in_specs=[pl.BlockSpec(memory_space=pltpu.SMEM), whole, whole, whole],
        out_specs=whole,
        scratch_shapes=[
            pltpu.VMEM(piece, jnp.bfloat16),
            pltpu.VMEM((slots + 1,) + piece[1:], jnp.bfloat16),
            pltpu.VMEM(piece, jnp.bfloat16),
            pltpu.VMEM((slots + 1, chunks, stat_rows, rows), jnp.float32),
            pltpu.VMEM((slots + 1, chunks, stat_rows, rows), jnp.float32),
            pltpu.VMEM((hops + 1, chunks, rows, width), jnp.float32),
            pltpu.VMEM((rows, width), jnp.float32),
            pltpu.VMEM((2, chunks, rows, width), jnp.bfloat16),
            pltpu.VMEM((2 * heads, HD), jnp.float32),
            pltpu.VMEM((2 * heads, HD), jnp.bfloat16),
            pltpu.VMEM((nb, 2 * heads, HD), jnp.bfloat16),
            pltpu.VMEM((nb, 2 * heads, HD), jnp.float32),
            pltpu.VMEM((2, nb, features), jnp.bfloat16),
            sems, sems, sems, sems, sems, sems,
            pltpu.SemaphoreType.DMA((nb,)),
            pltpu.SemaphoreType.DMA((nb,)),
            pltpu.SemaphoreType.DMA((2, chunks)),
            pltpu.SemaphoreType.DMA((2, chunks)),
        ],
        compiler_params=pltpu.CompilerParams(
            collective_id=0, has_side_effects=True, vmem_limit_bytes=60 * 2**20
        ),
        name="bar_attention",
    )(bar_lengths, queries, keys, values)


def solution(mesh):
    placed = (
        P(("groups", "ctx"), None),
        P(("groups", "ctx"), None),
        P(("groups", "ctx"), None),
        P("groups"),
    )
    return jax.shard_map(
        local, mesh=mesh, in_specs=placed, out_specs=P(("groups", "ctx"), None), check_vma=False
    )
```

```python
import functools
import math

import jax
import jax.numpy as jnp
from jax import lax
from jax.experimental import pallas as pl
from jax.experimental.pallas import tpu as pltpu
from jax.sharding import PartitionSpec as P

HD = 128
BAR_OFFSETS = (1, 2, 4, 8, 12, 16, 24, 32)
NEG_FILL = -1e30
LOG2E = math.log2(math.e)
SCALE = LOG2E / math.sqrt(HD)
CHUNKS = 8
EARLY = 1
LEND_EARLY = 0
LAG_NEAR = 0
LAG_EDGE = 1
LAG_FAR = 2
LAG_HOP = 1
STRIDE = 4


def kernel(
    nb, hops, chunks, len_ref, q_ref, k_ref, v_ref, o_ref,
    qin, oin, osend, lin, lloc, held, acc, low_kv, sum_f32, sum_send, sum_in, sum_wide, sum_rows,
    q_send, q_recv, o_send, o_recv, l_send, l_recv, s_send, s_recv, kv_send, kv_recv,
):
    rows, features = q_ref.shape
    heads = features // HD
    width = features // chunks
    per = width // HD
    near2, near1 = hops, hops + 1
    slots = hops + 2
    own, own_held, extra = slots, hops - 1, slots
    me = lax.axis_index("ctx")
    low_half = lax.rem(lax.div(me, 2), 2) == 0
    even = lax.rem(me, 2) == 0
    own_len = len_ref[me]
    lender = me < STRIDE
    borrower = (me >= STRIDE) & (me < 2 * STRIDE)
    inner = me >= 2 * STRIDE
    direct = lender & jnp.logical_not(low_half)

    def columns(c):
        return pl.ds(pl.multiple_of(c * width, width), width)

    def exists(slot):
        far = (me + STRIDE * (slot + 1) < nb) & jnp.logical_not(lender)
        return jnp.where(slot == near2, me + 2 < nb, jnp.where(slot == near1, me + 1 < nb, far))

    def parent(slot):
        two = jnp.where(low_half | direct, me + 2, me - 2)
        one = jnp.where(even, me + 1, me - 1)
        return jnp.where(slot == near2, two, jnp.where(slot == near1, one, me + STRIDE))

    def q_copy(src, slot, c, target, lane=None):
        return pltpu.make_async_remote_copy(
            src_ref=src, dst_ref=qin.at[slot, c], send_sem=q_send.at[slot if lane is None else lane, c],
            recv_sem=q_recv.at[slot, c], device_id={"ctx": target},
            device_id_type=pl.DeviceIdType.MESH,
        )

    def o_copies(slot, c, target, into=None):
        if into is None:
            into = jnp.where((slot == near2) & direct, extra, slot)
        return (
            pltpu.make_async_remote_copy(
                src_ref=osend.at[slot, c], dst_ref=oin.at[into, c], send_sem=o_send.at[slot, c],
                recv_sem=o_recv.at[into, c], device_id={"ctx": target},
                device_id_type=pl.DeviceIdType.MESH,
            ),
            pltpu.make_async_remote_copy(
                src_ref=lloc.at[slot, c], dst_ref=lin.at[into, c], send_sem=l_send.at[slot, c],
                recv_sem=l_recv.at[into, c], device_id={"ctx": target},
                device_id_type=pl.DeviceIdType.MESH,
            ),
        )

    def s_copy(target):
        return pltpu.make_async_remote_copy(
            src_ref=sum_send, dst_ref=sum_in.at[me], send_sem=s_send.at[target],
            recv_sem=s_recv.at[me], device_id={"ctx": target},
            device_id_type=pl.DeviceIdType.MESH,
        )

    sum_in[...] = jnp.zeros_like(sum_in)
    barrier = pltpu.get_barrier_semaphore()

    @pl.loop(0, nb)
    def _(j):
        @pl.when(j != me)
        def _():
            pl.semaphore_signal(
                barrier, inc=1, device_id={"ctx": j}, device_id_type=pl.DeviceIdType.MESH
            )

    live = (lax.broadcasted_iota(jnp.int32, (16, rows), 1) < own_len).astype(jnp.bfloat16)
    factor = lax.rsqrt(jnp.full((1, HD), own_len, jnp.int32).astype(jnp.float32))
    for part, ref in enumerate((k_ref, v_ref)):
        for h in range(heads):
            pooled = jnp.dot(
                live, ref[:, h * HD : (h + 1) * HD], preferred_element_type=jnp.float32
            )
            sum_f32[part * heads + h : part * heads + h + 1, :] = pooled[0:1, :] * factor
    sum_send[...] = sum_f32[...].astype(jnp.bfloat16)

    pl.semaphore_wait(barrier, nb - 1)

    def kv_copies(c):
        return [
            pltpu.make_async_remote_copy(
                src_ref=ref.at[:, columns(c)], dst_ref=low_kv.at[part, c],
                send_sem=kv_send.at[part, c], recv_sem=kv_recv.at[part, c],
                device_id={"ctx": me + STRIDE}, device_id_type=pl.DeviceIdType.MESH,
            )
            for part, ref in enumerate((k_ref, v_ref))
        ]

    def send_own(c):
        source = q_ref.at[:, columns(c)]

        @pl.when(inner)
        def _():
            q_copy(source, 0, c, me - STRIDE).start()

        @pl.when(borrower & low_half)
        def _():
            q_copy(source, near2, c, me - 2, extra).start()

        @pl.when(jnp.logical_not(low_half))
        def _():
            q_copy(source, near2, c, me - 2).start()

        @pl.when(jnp.logical_not(even))
        def _():
            q_copy(source, near1, c, me - 1).start()

    def lend(c):
        @pl.when(lender)
        def _():
            for copy in kv_copies(c):
                copy.start()

    for c in range(min(EARLY, chunks)):
        send_own(c)

    for c in range(min(LEND_EARLY, chunks)):
        lend(c)

    @pl.loop(0, nb)
    def _(j):
        @pl.when(j > me)
        def _():
            s_copy(j).start()

    def forward(c):
        for slot in range(slots):
            @pl.when(exists(slot))
            def _(slot=slot):
                q_copy(qin.at[slot, c], slot, c, parent(slot)).wait_recv()
                if slot + 1 < hops:
                    @pl.when(inner)
                    def _():
                        q_copy(qin.at[slot, c], slot + 1, c, me - STRIDE).start()
                if slot == 0:
                    @pl.when(low_half)
                    def _():
                        q_copy(qin.at[slot, c], near2, c, me + 2).start()
                if slot == near2:
                    @pl.when(even)
                    def _():
                        q_copy(qin.at[slot, c], near1, c, me + 1).start()

            if slot == hops - 1:
                @pl.when(c + EARLY < chunks)
                def _():
                    send_own(c + EARLY)

                @pl.when(c + LEND_EARLY < chunks)
                def _():
                    lend(c + LEND_EARLY)

    lane = lax.broadcasted_iota(jnp.int32, (rows, HD), 1)
    key_pos = lax.broadcasted_iota(jnp.int32, (1, rows), 1)
    live_bias = jnp.where(key_pos < own_len, 0.0, NEG_FILL).astype(jnp.float32)

    low_len = len_ref[jnp.maximum(me - STRIDE, 0)]
    low_bias = jnp.where(key_pos < low_len, 0.0, NEG_FILL).astype(jnp.float32)

    def listed(distance):
        return functools.reduce(jnp.logical_or, [distance == o for o in BAR_OFFSETS])

    def scores_of(q, k):
        return lax.dot_general(
            q, k, (((1,), (1,)), ((), ())), preferred_element_type=jnp.float32
        ) * SCALE

    def head_columns(c, h):
        return pl.ds(pl.multiple_of(c * width + h * HD, HD), HD)

    def keep_state(levels, totals, slot, c):
        inverse = 1.0 / totals
        for h in range(per):
            here = slice(h * HD, (h + 1) * HD)
            acc[:, here] = acc[:, here] * inverse[:, h : h + 1]
        log_sums = levels + jnp.log(totals) * LOG2E
        lloc[slot, c] = jnp.transpose(log_sums)[: lloc.shape[2], :]

    def local_peer(slot, c):
        m_all = jnp.zeros((rows, HD), jnp.float32)
        l_all = jnp.ones((rows, HD), jnp.float32)
        for h in range(per):
            here = slice(h * HD, (h + 1) * HD)
            s = scores_of(qin[slot, c, :, here], k_ref[:, head_columns(c, h)]) + live_bias
            m = jnp.max(s, axis=1, keepdims=True)
            p = jnp.exp2(s - m)
            l = jnp.sum(p, axis=1, keepdims=True)
            acc[:, here] = jnp.dot(
                p.astype(jnp.bfloat16), v_ref[:, head_columns(c, h)],
                preferred_element_type=jnp.float32,
            )
            m_all = jnp.where(lane == h, m, m_all)
            l_all = jnp.where(lane == h, l, l_all)
        keep_state(m_all, l_all, slot, c)

    def local_two(slot, c):
        near_bias = live_bias + jnp.where(listed(STRIDE * (slot + 1)), 0.0, NEG_FILL)
        far_bias = low_bias + jnp.where(listed(STRIDE * (slot + 2)), 0.0, NEG_FILL)
        m_all = jnp.zeros((rows, HD), jnp.float32)
        l_all = jnp.ones((rows, HD), jnp.float32)
        for h in range(per):
            here = slice(h * HD, (h + 1) * HD)
            q = qin[slot, c, :, here]
            s = scores_of(q, k_ref[:, head_columns(c, h)]) + near_bias
            t = scores_of(q, low_kv[0, c, :, here]) + far_bias
            m = jnp.max(jnp.maximum(s, t), axis=1, keepdims=True)
            p = jnp.exp2(s - m)
            r = jnp.exp2(t - m)
            l = jnp.sum(p + r, axis=1, keepdims=True)
            acc[:, here] = jnp.dot(
                p.astype(jnp.bfloat16), v_ref[:, head_columns(c, h)],
                preferred_element_type=jnp.float32,
            ) + jnp.dot(
                r.astype(jnp.bfloat16), low_kv[1, c, :, here],
                preferred_element_type=jnp.float32,
            )
            m_all = jnp.where(lane == h, m, m_all)
            l_all = jnp.where(lane == h, l, l_all)
        keep_state(m_all, l_all, slot, c)

    def local_own(c, two):
        causal = (
            lax.broadcasted_iota(jnp.int32, (rows, rows), 1)
            <= lax.broadcasted_iota(jnp.int32, (rows, rows), 0)
        ) & (key_pos < own_len)
        bars = lax.broadcasted_iota(jnp.int32, (1, nb), 1)
        coarse = bars < me
        for offset in BAR_OFFSETS:
            coarse = coarse & (bars != me - offset)
        coarse_bias = jnp.where(coarse, 0.0, NEG_FILL).astype(jnp.float32)
        m_all = jnp.zeros((rows, HD), jnp.float32)
        l_all = jnp.ones((rows, HD), jnp.float32)
        for h in range(per):
            here = slice(h * HD, (h + 1) * HD)
            q = q_ref[:, head_columns(c, h)]
            s = jnp.where(causal, scores_of(q, k_ref[:, head_columns(c, h)]), NEG_FILL)
            t = scores_of(q, sum_rows[0, :, head_columns(c, h)]) + coarse_bias
            m = jnp.maximum(
                jnp.max(s, axis=1, keepdims=True), jnp.max(t, axis=1, keepdims=True)
            )
            if two:
                u = scores_of(q, low_kv[0, c, :, here]) + low_bias
                m = jnp.maximum(m, jnp.max(u, axis=1, keepdims=True))
            p = jnp.exp2(s - m)
            r = jnp.exp2(t - m)
            l = jnp.sum(p, axis=1, keepdims=True) + jnp.sum(r, axis=1, keepdims=True)
            mixed = jnp.dot(
                p.astype(jnp.bfloat16), v_ref[:, head_columns(c, h)],
                preferred_element_type=jnp.float32,
            ) + jnp.dot(
                r.astype(jnp.bfloat16), sum_rows[1, :, head_columns(c, h)],
                preferred_element_type=jnp.float32,
            )
            if two:
                w = jnp.exp2(u - m)
                l = l + jnp.sum(w, axis=1, keepdims=True)
                mixed = mixed + jnp.dot(
                    w.astype(jnp.bfloat16), low_kv[1, c, :, here],
                    preferred_element_type=jnp.float32,
                )
            acc[:, here] = mixed
            m_all = jnp.where(lane == h, m, m_all)
            l_all = jnp.where(lane == h, l, l_all)
        keep_state(m_all, l_all, own, c)
        held[own_held, c] = acc[...]

    def merge(child, held_slot, slot, c):
        for copy in o_copies(min(child, near1), c, parent(min(child, near1)), child):
            copy.wait_recv()
        mine, theirs = lloc[slot, c], lin[child, c]
        top = jnp.maximum(mine, theirs)
        both = top + jnp.log(jnp.exp2(mine - top) + jnp.exp2(theirs - top)) * LOG2E
        lloc[slot, c] = both
        shares = jnp.transpose(
            jnp.concatenate(
                [
                    jnp.exp2(mine - both),
                    jnp.exp2(theirs - both),
                    jnp.zeros((HD - 2 * mine.shape[0], rows), jnp.float32),
                ],
                axis=0,
            )
        )
        second = mine.shape[0]
        for h in range(per):
            here = slice(h * HD, (h + 1) * HD)
            held[held_slot, c, :, here] = (
                held[held_slot, c, :, here] * shares[:, h : h + 1]
                + oin[child, c, :, here].astype(jnp.float32) * shares[:, second + h : second + h + 1]
            )

    def send_state(state, slot, c):
        osend[slot, c] = state.astype(jnp.bfloat16)
        for copy in o_copies(slot, c, parent(slot)):
            copy.start()

    idle_hops = [s for s in range(hops) if STRIDE * (s + 1) not in BAR_OFFSETS]
    far_child = inner

    def local_answer(slot, c):
        double = borrower & (slot < hops)

        @pl.when(double)
        def _():
            local_two(slot, c)

        if idle_hops:
            idle = functools.reduce(jnp.logical_or, [slot == s for s in idle_hops])
            idle = idle & jnp.logical_not(double)

            @pl.when(idle)
            def _():
                acc[...] = jnp.zeros_like(acc)
                lloc[slot, c] = jnp.full(lloc.shape[2:], NEG_FILL, jnp.float32)

            @pl.when(jnp.logical_not(idle | double))
            def _():
                local_peer(slot, c)
        else:
            @pl.when(jnp.logical_not(double))
            def _():
                local_peer(slot, c)

        has_child = (
            ((slot + 1 < hops) & far_child) | ((slot == 0) & low_half) | ((slot == near2) & even)
        )

        @pl.when(jnp.logical_not(has_child))
        def _():
            send_state(acc[...], slot, c)

        @pl.when(has_child)
        def _():
            held[slot, c] = acc[...]

    def finish(c):
        @pl.when(far_child)
        def _():
            merge(0, own_held, own, c)

        @pl.when(jnp.logical_not(low_half))
        def _():
            merge(near2, own_held, own, c)

        @pl.when(jnp.logical_not(even))
        def _():
            merge(near1, own_held, own, c)

        @pl.when(borrower & low_half)
        def _():
            merge(extra, own_held, own, c)

        used = lax.broadcasted_iota(jnp.int32, (rows, HD), 0) < own_len
        for h in range(per):
            here = slice(h * HD, (h + 1) * HD)
            o_ref[:, head_columns(c, h)] = jnp.where(
                used, held[own_held, c, :, here], 0.0
            ).astype(o_ref.dtype)

    @pl.loop(0, nb)
    def _(j):
        @pl.when(j < me)
        def _():
            pltpu.make_async_remote_copy(
                src_ref=sum_send, dst_ref=sum_in.at[j], send_sem=s_send.at[j],
                recv_sem=s_recv.at[j], device_id={"ctx": j},
                device_id_type=pl.DeviceIdType.MESH,
            ).wait_recv()

    sum_wide[...] = sum_in[...].astype(jnp.float32)
    for part in range(2):
        for h in range(heads):
            sum_rows[part, :, h * HD : (h + 1) * HD] = sum_wide[:, part * heads + h, :].astype(
                jnp.bfloat16
            )

    far_lags = [LAG_FAR + LAG_HOP * (hops - 2 - s) for s in range(hops - 1)]
    own_lag = (far_lags[0] if far_lags else LAG_FAR) + LAG_HOP

    @pl.loop(0, chunks + 1 + own_lag)
    def _(step):
        def at(lag, also, body):
            c = step - 1 - lag

            @pl.when((c >= 0) & (c < chunks) & also)
            def _():
                body(c)

        @pl.when(step < chunks)
        def _():
            forward(step)

        @pl.when((step >= 1) & (step <= chunks))
        def _():
            @pl.when(borrower)
            def _():
                for copy in kv_copies(step - 1):
                    copy.wait_recv()

            @pl.loop(0, slots)
            def _(j):
                slot = slots - 1 - j

                @pl.when(exists(slot))
                def _():
                    local_answer(slot, step - 1)

            @pl.when(borrower)
            def _():
                local_own(step - 1, True)

            @pl.when(jnp.logical_not(borrower))
            def _():
                local_own(step - 1, False)

        def near_answer(c):
            merge(near1, near2, near2, c)
            send_state(held[near2, c], near2, c)

        at(LAG_NEAR, exists(near2) & even, near_answer)

        for s in reversed(range(hops)):
            def far_answer(c, s=s):
                merge(s + 1, s, s, c)
                if s == 0:
                    @pl.when(low_half)
                    def _():
                        merge(near2, s, s, c)
                send_state(held[s, c], s, c)

            def edge_answer(c):
                merge(near2, 0, 0, c)
                send_state(held[0, c], 0, c)

            if s < hops - 1:
                at(far_lags[s], exists(s) & far_child, far_answer)
            if s == 0:
                alone = low_half if hops == 1 else low_half & jnp.logical_not(far_child)
                at(LAG_EDGE, exists(0) & alone, edge_answer)

        at(own_lag, me >= 0, finish)

    @pl.loop(0, nb)
    def _(j):
        @pl.when(j > me)
        def _():
            s_copy(j).wait_send()

    @pl.loop(0, chunks)
    def _(c):
        @pl.when(borrower & low_half)
        def _():
            q_copy(qin.at[near2, c], near2, c, me - 2, extra).wait_send()

        @pl.when(lender)
        def _():
            for copy in kv_copies(c):
                copy.wait_send()

        for slot in range(slots):
            if slot == 0:
                sent = inner
            elif slot < hops:
                sent = inner & (me + STRIDE * slot < nb)
            elif slot == near2:
                sent = jnp.logical_not(low_half) | ((me + STRIDE < nb) & jnp.logical_not(lender))
            else:
                sent = jnp.logical_not(even) | (me + 2 < nb)

            @pl.when(sent)
            def _(slot=slot):
                q_copy(qin.at[slot, c], slot, c, parent(slot)).wait_send()

            @pl.when(exists(slot))
            def _(slot=slot):
                for copy in o_copies(slot, c, parent(slot)):
                    copy.wait_send()


def local(queries, keys, values, bar_lengths):
    nb = lax.axis_size("ctx")
    rows, features = queries.shape
    heads = features // HD
    chunks = CHUNKS
    width = features // chunks
    hops = max(o // STRIDE for o in BAR_OFFSETS if o % STRIDE == 0 and o < nb)
    hops = min(hops, nb // STRIDE - 2)
    slots = hops + 2
    stat_rows = 8
    piece = (slots, chunks, rows, width)
    sems = pltpu.SemaphoreType.DMA((slots + 1, chunks))
    whole = pl.BlockSpec(memory_space=pltpu.VMEM)
    return pl.pallas_call(
        functools.partial(kernel, nb, hops, chunks),
        out_shape=jax.ShapeDtypeStruct((rows, features), jnp.bfloat16),
        in_specs=[pl.BlockSpec(memory_space=pltpu.SMEM), whole, whole, whole],
        out_specs=whole,
        scratch_shapes=[
            pltpu.VMEM(piece, jnp.bfloat16),
            pltpu.VMEM((slots + 1,) + piece[1:], jnp.bfloat16),
            pltpu.VMEM(piece, jnp.bfloat16),
            pltpu.VMEM((slots + 1, chunks, stat_rows, rows), jnp.float32),
            pltpu.VMEM((slots + 1, chunks, stat_rows, rows), jnp.float32),
            pltpu.VMEM((hops + 1, chunks, rows, width), jnp.float32),
            pltpu.VMEM((rows, width), jnp.float32),
            pltpu.VMEM((2, chunks, rows, width), jnp.bfloat16),
            pltpu.VMEM((2 * heads, HD), jnp.float32),
            pltpu.VMEM((2 * heads, HD), jnp.bfloat16),
            pltpu.VMEM((nb, 2 * heads, HD), jnp.bfloat16),
            pltpu.VMEM((nb, 2 * heads, HD), jnp.float32),
            pltpu.VMEM((2, nb, features), jnp.bfloat16),
            sems, sems, sems, sems, sems, sems,
            pltpu.SemaphoreType.DMA((nb,)),
            pltpu.SemaphoreType.DMA((nb,)),
            pltpu.SemaphoreType.DMA((2, chunks)),
            pltpu.SemaphoreType.DMA((2, chunks)),
        ],
        compiler_params=pltpu.CompilerParams(
            collective_id=0, has_side_effects=True, vmem_limit_bytes=60 * 2**20
        ),
        name="bar_attention",
    )(bar_lengths, queries, keys, values)


def solution(mesh):
    placed = (
        P(("groups", "ctx"), None),
        P(("groups", "ctx"), None),
        P(("groups", "ctx"), None),
        P("groups"),
    )
    return jax.shard_map(
        local, mesh=mesh, in_specs=placed, out_specs=P(("groups", "ctx"), None), check_vma=False
    )
```
